32 devices in a mesh: groups: 2 (over y), chan: 4 (over z), space: 2 (over x), pair: 2 (over core).
Axes of the slice: x: 2, y: 2, z: 4, core: 2. Of those that a mesh axis runs over, the one named last changes fastest.
Arguments:
- grad_out: bfloat16 [512, 32, 1024], P('chan', ('groups', 'space', 'pair')), parts along dimension 1, may hold values from -6 to 6
- conv_weight: bfloat16 [27, 512, 512], P(None, 'chan'), may hold values from -0.0546875 to 0.0546875
- pre_act: bfloat16 [32, 1024, 512], P(('groups', 'space', 'pair'), 'chan'), parts along dimension 0, may hold values from -6 to 6
- down_weight: bfloat16 [8, 256, 512], replicated, may hold values from -0.25 to 0.25
Outputs:
- grad_fine: bfloat16 [32, 1024, 8, 256], P(('groups', 'space', 'pair'), 'chan'), parts along dimension 0
The draws below stay inside these ranges and needn't reach their ends.
There are 2 independent parts, one for each index of `groups`. The reference program is written for one: setup_inputs(seed, part) draws one part's arguments, and reference() takes and returns one part's arrays. A program takes and returns all parts, laid end to end along the dimension named above; an argument that names none is the same for every part. Nothing has to cross between parts.
All inputs are finite; a program needn't handle non-finite values.
Results may differ from the reference program's by a relative error of at most 0.025.
Values may be sent and summed in bfloat16 or wider, within the bound.
A program may use at most 64 MiB of HBM per device.

```python
import math
import jax
import jax.numpy as jnp
from jax import lax

C = 512
CF = 256
NZ = 8
NX = 16
PLANE = 1024
N_CHAN = 4


def block_levels(own_key, shape, split, low, largest):
    def one(axis_at, parts):
        steps = jax.random.uniform(jax.random.fold_in(jax.random.fold_in(own_key, 6), axis_at), (parts,), jnp.float32, low / len(split), largest / len(split))
        return jnp.repeat(jnp.exp(steps), shape[axis_at] // parts).reshape((-1,) + (1,) * (len(shape) - axis_at - 1))

    gain = one(*split[0])
    for cut in split[1:]:
        gain = gain * one(*cut)
    return gain


def noise(rng, shape, width, bound, cuts=(), kind=jnp.bfloat16):
    values = jax.random.normal(rng, shape, jnp.float32) * width
    if len(cuts) > 0:
        values = block_levels(rng, shape, cuts, -0.22, 0.18) * values
    return jnp.clip(values, min=-bound, max=bound).astype(kind)


def setup_inputs(seed: int = 0, part: int = 0) -> dict:
    splits = jax.random.split(jax.random.key(seed), 5)
    part_splits = jax.random.split(jax.random.fold_in(splits[4], part), 5)
    return {
        "grad_out": noise(part_splits[0], (C, NX, PLANE), 1.0, 6.0, ((0, 4), (1, 4))),
        "conv_weight": noise(splits[1], (27, C, C), (27 * C) ** -0.5, 0.0546875, ((1, 4),)),
        "pre_act": noise(part_splits[2], (NX, PLANE, C), 1.5, 6.0, ((0, 4), (1, 4))),
        "down_weight": noise(splits[3], (8, CF, C), C ** -0.5, 0.25),
    }


def shifted_stack(padded, depth):
    extent = padded.shape[1] - 2
    plane_len = padded.shape[2]
    widened = jnp.pad(padded, ((0, 0), (0, 0), (depth + 1, depth + 1)))
    z_index = jnp.arange(plane_len, dtype=jnp.int32) % depth
    pieces = []
    for step_x in (-1, 0, 1):
        x_rows = widened[:, 1 - step_x:1 - step_x + extent, :]
        for step_y in (-1, 0, 1):
            for step_z in (-1, 0, 1):
                offset = step_y * depth + step_z
                piece = x_rows[:, :, depth + 1 - offset:depth + 1 - offset + plane_len]
                inside = (z_index - step_z >= 0) & (z_index - step_z < depth)
                pieces.append(jnp.where(inside, piece, jnp.zeros_like(piece)))
    return jnp.stack(pieces)

def gelu_slope(values):
    return 0.5 * (1.0 + jax.scipy.special.erf(values / math.sqrt(2.0))) + values * jnp.exp(-0.5 * values * values) / math.sqrt(2.0 * math.pi)

def reference(grad_out, conv_weight, pre_act, down_weight):
    extent = grad_out.shape[1]
    padded = jnp.pad(grad_out, ((0, 0), (1, 1), (0, 0)))
    per_block = C // N_CHAN

    def block_term(carry, index):
        start = (index * per_block).astype(jnp.int32)
        block_grad = lax.dynamic_slice_in_dim(padded, start, per_block, 0)
        block_weight = lax.dynamic_slice_in_dim(conv_weight, start, per_block, 1)
        stacked = shifted_stack(block_grad, NZ)
        term = jnp.einsum('dokp,doi->kpi', stacked.astype(jnp.float32), block_weight.astype(jnp.float32))
        term = lax.optimization_barrier(term.astype(jnp.bfloat16)).astype(jnp.float32)
        return (carry + term, None)
    total, unused = lax.scan(block_term, jnp.zeros((extent, PLANE, C), jnp.float32), jnp.arange(N_CHAN, dtype=jnp.int32))
    grad_act = total.astype(jnp.bfloat16)
    values = pre_act.astype(jnp.float32)
    grad_pre = (grad_act.astype(jnp.float32) * gelu_slope(values)).astype(jnp.bfloat16)
    result = jnp.einsum('xpk,efk->xpef', grad_pre.astype(jnp.float32), down_weight.astype(jnp.float32))
    return result.astype(jnp.bfloat16)
```

```python
import functools
import math

import jax
import jax.numpy as jnp
from jax import lax
from jax.experimental import pallas as pl
from jax.experimental.pallas import tpu as pltpu
from jax.sharding import PartitionSpec as P

NZ = 8
MESH = pl.DeviceIdType.MESH


def with_halo(cells, sides, width):
    for axis, dim in sides:
        count = lax.axis_size(axis)
        ends = count - 1
        head = lax.slice_in_dim(cells, 0, width, axis=dim)
        tail = lax.slice_in_dim(cells, cells.shape[dim] - width, cells.shape[dim], axis=dim)
        cells = jnp.concatenate(
            [
                lax.ppermute(tail, axis, [(i, (i + 1) % count) for i in range(ends)]),
                cells,
                lax.ppermute(head, axis, [((i + 1) % count, i) for i in range(ends)]),
            ],
            axis=dim,
        )
    return cells


def shifted_stack(padded, depth):
    extent = padded.shape[1] - 2
    plane_len = padded.shape[2]
    widened = jnp.pad(padded, ((0, 0), (0, 0), (depth + 1, depth + 1)))
    z_index = jnp.arange(plane_len, dtype=jnp.int32) % depth
    pieces = []
    for step_x in (-1, 0, 1):
        x_rows = widened[:, 1 - step_x : 1 - step_x + extent, :]
        for step_y in (-1, 0, 1):
            for step_z in (-1, 0, 1):
                offset = step_y * depth + step_z
                piece = x_rows[:, :, depth + 1 - offset : depth + 1 - offset + plane_len]
                inside = (z_index - step_z >= 0) & (z_index - step_z < depth)
                pieces.append(jnp.where(inside, piece, jnp.zeros_like(piece)))
    return jnp.stack(pieces)


def gelu_slope(values):
    return 0.5 * (1.0 + jax.scipy.special.erf(values / math.sqrt(2.0))) + values * jnp.exp(
        -0.5 * values * values
    ) / math.sqrt(2.0 * math.pi)


def finish(grad_act, pre_act, down_weight):
    values = pre_act.astype(jnp.float32)
    grad_pre = (grad_act.astype(jnp.float32) * gelu_slope(values)).astype(jnp.bfloat16)
    result = lax.dot_general(
        grad_pre, down_weight, (((2,), (2,)), ((), ())), preferred_element_type=jnp.float32
    )
    return result.astype(jnp.bfloat16)


def body_blocks(grad_out, conv_weight, pre_act, down_weight):
    padded = with_halo(grad_out, ((("space", "pair"), 1),), 1)
    stacked = shifted_stack(padded, NZ)
    partial_sum = lax.dot_general(
        stacked, conv_weight, (((0, 1), (0, 1)), ((), ())), preferred_element_type=jnp.float32
    )
    grad_act = lax.psum_scatter(
        partial_sum.astype(jnp.bfloat16), "chan", scatter_dimension=1, tiled=True
    )
    return finish(grad_act, pre_act, down_weight)


def conv_kernel(
    n, ns, nx, ny, s_ref, w_ref, out_ref,
    w_all, cells, shifted, acc,
    w_send, w_recv, g_send, g_recv, h_send, h_recv, local,
):
    gy, z = lax.axis_index("groups"), lax.axis_index("chan")
    sx, core = lax.axis_index("space"), lax.axis_index("pair")
    main = NZ * ny
    taps, rows, piece_rows = 27, w_all.shape[1], w_all.shape[1] // 8
    to_x = {"space": sx + 1 - 2 * lax.rem(sx, 2)}
    to_y = {"groups": 1 - gy}
    to_core = {"pair": 1 - core}
    cross_space = sx + 2 * core - 1
    to_cross = {"space": cross_space, "pair": 1 - core}
    has_cross = (cross_space >= 0) & (cross_space < ns)
    q = gy * 4 + lax.rem(sx, 2) * 2 + core

    def flip(index, gy_flip, x_flip, core_flip):
        g = 1 - gy if gy_flip else gy
        x = 1 - lax.rem(sx, 2) if x_flip else lax.rem(sx, 2)
        c = 1 - core if core_flip else core
        return g * 4 + x * 2 + c

    q_x, q_y, q_d = flip(q, 0, 1, 0), flip(q, 1, 0, 0), flip(q, 1, 1, 0)
    pieces = (q, q_x, q_y, q_d)
    partner_pieces = (flip(q, 0, 0, 1), flip(q, 0, 1, 1), flip(q, 1, 0, 1), flip(q, 1, 1, 1))

    barrier = pltpu.get_barrier_semaphore()
    for hop in range(1, n):
        pl.semaphore_signal(
            barrier, inc=1, device_id={"chan": lax.rem(z + hop, n)}, device_id_type=MESH
        )
    for target in (to_x, to_y, to_core):
        pl.semaphore_signal(barrier, inc=1, device_id=target, device_id_type=MESH)

    @pl.when(has_cross)
    def _():
        pl.semaphore_signal(barrier, inc=1, device_id=to_cross, device_id_type=MESH)

    own_w = pltpu.make_async_copy(w_ref, w_all.at[z], local.at[0])
    own_g = pltpu.make_async_copy(s_ref.at[z], cells.at[z, pl.ds(1, nx)], local.at[1])
    own_w.start()
    own_g.start()

    @pl.when(has_cross)
    def _():
        pl.semaphore_wait(barrier, n + 3)

    @pl.when(jnp.logical_not(has_cross))
    def _():
        pl.semaphore_wait(barrier, n + 2)

    def w_rows(piece):
        return pl.ds(pl.multiple_of(piece * piece_rows, piece_rows), piece_rows)

    def w_copy(kind, way, step, shard, piece, target):
        view = w_all.at[shard, w_rows(piece)]
        return pltpu.make_async_remote_copy(
            src_ref=view, dst_ref=view,
            send_sem=w_send.at[kind, way, step], recv_sem=w_recv.at[kind, way, step],
            device_id=target, device_id_type=MESH,
        )

    def own_z_copy(way):
        return pltpu.make_async_remote_copy(
            src_ref=w_ref.at[w_rows(q)], dst_ref=w_all.at[z, w_rows(q)],
            send_sem=w_send.at[0, way, 1], recv_sem=w_recv.at[0, way, 1],
            device_id={"chan": z + 1 - 2 * way}, device_id_type=MESH,
        )

    def g_copy(way, step):
        target = z + step * (1 - 2 * way)
        return pltpu.make_async_remote_copy(
            src_ref=s_ref.at[target], dst_ref=cells.at[z, pl.ds(1, nx)],
            send_sem=g_send.at[way, step], recv_sem=g_recv.at[way, step],
            device_id={"chan": target}, device_id_type=MESH,
        )

    def g_arrival(way, step):
        shard = z - step * (1 - 2 * way)
        return pltpu.make_async_remote_copy(
            src_ref=s_ref.at[z], dst_ref=cells.at[shard, pl.ds(1, nx)],
            send_sem=g_send.at[way, step], recv_sem=g_recv.at[way, step],
            device_id={"chan": shard}, device_id_type=MESH,
        )

    def h_copy(side, way, step, shard, sending):
        last = nx + 1
        if side == 0:
            source, landing, target = nx - (nx - 1) * core, last * core, to_core
            arriving = last * (1 - core)
        else:
            source, landing, target = 1 + (nx - 1) * core, last * (1 - core), to_cross
            arriving = last * core
        return pltpu.make_async_remote_copy(
            src_ref=cells.at[shard, source],
            dst_ref=cells.at[shard, landing if sending else arriving],
            send_sem=h_send.at[side, way, step], recv_sem=h_recv.at[side, way, step],
            device_id=target, device_id_type=MESH,
        )

    def sends_on(way, step):
        return z + step < n if way == 0 else z - step >= 0

    def arrives(way, step):
        return z - step >= 0 if way == 0 else z + step < n

    def shard_of(way, step):
        return z - step if way == 0 else z + step

    def each_arrival(step, act):
        for way in (0, 1):
            @pl.when(arrives(way, step))
            def _():
                act(way, step, shard_of(way, step))

    for step in range(1, n):
        for way in (0, 1):
            @pl.when(sends_on(way, step))
            def _():
                g_copy(way, step).start()
                if step == 1:
                    own_z_copy(way).start()

    def start_halo(way, step, shard):
        h_copy(0, way, step, shard, True).start()

        @pl.when(has_cross)
        def _():
            h_copy(1, way, step, shard, True).start()

        @pl.when(jnp.logical_not(has_cross))
        def _():
            cells[shard, (nx + 1) * core] = jnp.zeros(cells.shape[2:], cells.dtype)

    def end_halo(way, step, shard):
        h_copy(0, way, step, shard, False).wait_recv()

        @pl.when(has_cross)
        def _():
            h_copy(1, way, step, shard, False).wait_recv()

        def plane(x, carry):
            values = cells[shard, x, pl.ds(0, main)]
            edge = cells[shard, x, pl.ds(main, 2 * NZ)].astype(jnp.float32)
            wide = values.astype(jnp.float32)
            width = wide.shape[1]
            row = lax.broadcasted_iota(jnp.int32, (main, width), 0) % ny
            low = jnp.broadcast_to(edge[:NZ][:, None, :], (NZ, ny, width)).reshape(main, width)
            high = jnp.broadcast_to(edge[NZ:][:, None, :], (NZ, ny, width)).reshape(main, width)
            after = jnp.where(row == ny - 1, high, pltpu.roll(wide, main - 1, 0))
            before = jnp.where(row == 0, low, pltpu.roll(wide, 1, 0))
            shifted[0, shard, x, pl.ds(ny, main)] = after.astype(jnp.bfloat16)
            shifted[1, shard, x, pl.ds(ny, main)] = values
            shifted[2, shard, x, pl.ds(ny, main)] = before.astype(jnp.bfloat16)
            blank = jnp.zeros((ny, width), jnp.bfloat16)
            for kind in range(3):
                shifted[kind, shard, x, pl.ds(0, ny)] = blank
                shifted[kind, shard, x, pl.ds(ny + main, ny)] = blank
            return carry

        lax.fori_loop(0, nx + 2, plane, 0)

    def stage_a(way, step, shard):
        w_copy(0, way, step, shard, q, to_core).wait_recv()
        w_copy(5, way, step, shard, q, to_x).start()
        w_copy(6, way, step, shard, q, to_y).start()
        if step < n - 1:
            @pl.when(sends_on(way, 1))
            def _():
                w_copy(0, way, step + 1, shard, q, {"chan": z + 1 - 2 * way}).start()
        w_copy(1, way, step, shard, q, to_core).start()
        g_arrival(way, step).wait_recv()
        start_halo(way, step, shard)

    def stage_b(way, step, shard):
        w_copy(5, way, step, shard, q_x, to_x).wait_recv()

        @pl.when(core == 0)
        def _():
            w_copy(7, way, step, shard, q_x, to_y).start()

        w_copy(2, way, step, shard, q_x, to_core).start()
        w_copy(6, way, step, shard, q_y, to_y).wait_recv()

        @pl.when(core == 1)
        def _():
            w_copy(7, way, step, shard, q_y, to_x).start()

        w_copy(3, way, step, shard, q_y, to_core).start()

    def stage_c(way, step, shard):
        w_copy(7, way, step, shard, q_d, to_y).wait_recv()
        w_copy(4, way, step, shard, q_d, to_core).start()

    def multiply(shard, first):
        width = cells.shape[3]
        weights = w_all.at[shard]

        def planes(half, carry):
            parts = []
            for step_x in (-1, 0, 1):
                for step_y in (-1, 0, 1):
                    for step_z in (-1, 0, 1):
                        part = shifted[
                            step_y + 1, shard, pl.ds(half * 2 + 1 - step_x, 2),
                            pl.ds((1 - step_z) * ny, main),
                        ]
                        parts.append(part.reshape(2 * main, width))
            product = jnp.dot(
                jnp.concatenate(parts, axis=1), weights[...],
                preferred_element_type=jnp.float32,
            ).reshape(2, main, out_ref.shape[2])
            if first:
                acc[pl.ds(half * 2, 2)] = product
            else:
                acc[pl.ds(half * 2, 2)] += product
            return carry

        lax.fori_loop(0, nx // 2, planes, 0)

    def compute(way, step, shard):
        end_halo(way, step, shard)
        for kind in range(4):
            w_copy(1 + kind, way, step, shard, partner_pieces[kind], to_core).wait_recv()
        multiply(shard, False)

    own_g.wait()
    start_halo(0, 0, z)
    own_w.wait()
    end_halo(0, 0, z)
    each_arrival(1, stage_a)
    multiply(z, True)
    for step in range(1, n):
        each_arrival(step, stage_b)
        if step + 1 < n:
            each_arrival(step + 1, stage_a)
        each_arrival(step, stage_c)
        each_arrival(step, compute)
    out_ref[...] = acc[...].astype(out_ref.dtype)

    def end_sends(way, step, shard):
        w_copy(5, way, step, shard, q, to_x).wait_send()
        w_copy(6, way, step, shard, q, to_y).wait_send()
        for kind in range(4):
            w_copy(1 + kind, way, step, shard, pieces[kind], to_core).wait_send()

        @pl.when(core == 0)
        def _():
            w_copy(7, way, step, shard, q_x, to_y).wait_send()

        @pl.when(core == 1)
        def _():
            w_copy(7, way, step, shard, q_y, to_x).wait_send()

        if step < n - 1:
            @pl.when(sends_on(way, 1))
            def _():
                w_copy(0, way, step + 1, shard, q, {"chan": z + 1 - 2 * way}).wait_send()
        end_halo_sends(way, step, shard)

    def end_halo_sends(way, step, shard):
        h_copy(0, way, step, shard, True).wait_send()

        @pl.when(has_cross)
        def _():
            h_copy(1, way, step, shard, True).wait_send()

    end_halo_sends(0, 0, z)
    for step in range(1, n):
        each_arrival(step, end_sends)
        for way in (0, 1):
            @pl.when(sends_on(way, step))
            def _():
                g_copy(way, step).wait_send()
                if step == 1:
                    own_z_copy(way).wait_send()


def body_gather(n, ns, grad_out, conv_weight, pre_act, down_weight):
    channels, nx, plane = grad_out.shape
    rows_y = plane // NZ
    ny = rows_y // n
    wide = conv_weight.shape[2]
    main = NZ * ny
    turned = grad_out.reshape(channels, nx, rows_y, NZ).transpose(1, 3, 2, 0)
    edged = jnp.pad(turned, ((0, 0), (0, 0), (1, 1), (0, 0)))
    blocks = turned.reshape(nx, NZ, n, ny, channels).transpose(2, 0, 1, 3, 4)
    blocks = blocks.reshape(n, nx, main, channels)
    low = edged[:, :, 0 : rows_y : ny].transpose(2, 0, 1, 3)
    high = edged[:, :, ny + 1 :: ny].transpose(2, 0, 1, 3)
    send = jnp.concatenate([blocks, low, high], axis=2)
    weights = conv_weight.reshape(-1, wide)
    vmem = pltpu.VMEM
    dma = pltpu.SemaphoreType.DMA
    grad_act = pl.pallas_call(
        functools.partial(conv_kernel, n, ns, nx, ny),
        out_shape=jax.ShapeDtypeStruct((nx, main, wide), jnp.bfloat16),
        in_specs=[pl.BlockSpec(memory_space=pl.ANY)] * 2,
        out_specs=pl.BlockSpec(memory_space=pltpu.VMEM),
        scratch_shapes=[
            vmem((n, weights.shape[0], wide), jnp.bfloat16),
            vmem((n, nx + 2, main + 2 * NZ, channels), jnp.bfloat16),
            vmem((3, n, nx + 2, main + 2 * ny, channels), jnp.bfloat16),
            vmem((nx, main, wide), jnp.float32),
            dma((8, 2, n)), dma((8, 2, n)),
            dma((2, n)), dma((2, n)),
            dma((2, 2, n)), dma((2, 2, n)),
            dma((2,)),
        ],
        compiler_params=pltpu.CompilerParams(
            collective_id=0, has_side_effects=True, vmem_limit_bytes=56 * 2**20
        ),
        cost_estimate=pl.CostEstimate(
            flops=2 * 27 * n * channels * nx * main * wide,
            bytes_accessed=8 * 2**20, transcendentals=0,
        ),
    )(send, weights)
    grad_act = grad_act.reshape(nx, NZ, ny, wide).transpose(0, 2, 1, 3).reshape(nx, main, wide)
    return finish(grad_act, pre_act, down_weight)


def solution(mesh):
    in_specs = (
        P("chan", ("groups", "space", "pair"), None),
        P(None, "chan", None),
        P(("groups", "space", "pair"), "chan", None),
        P(),
    )
    out_specs = P(("groups", "space", "pair"), "chan", None, None)
    n, ns = mesh.shape["chan"], mesh.shape["space"]

    def body(grad_out, conv_weight, pre_act, down_weight):
        channels, nx, plane = grad_out.shape
        ny = plane // NZ // n
        fits = channels % 128 == 0 and ny % 16 == 0 and nx % 2 == 0 and ns % 2 == 0
        fits = fits and mesh.shape["groups"] == 2 and mesh.shape["pair"] == 2
        if fits:
            return body_gather(n, ns, grad_out, conv_weight, pre_act, down_weight)
        return body_blocks(grad_out, conv_weight, pre_act, down_weight)

    return jax.shard_map(body, mesh=mesh, in_specs=in_specs, out_specs=out_specs, check_vma=False)
```

```python
import functools
import math

import jax
import jax.numpy as jnp
from jax import lax
from jax.experimental import pallas as pl
from jax.experimental.pallas import tpu as pltpu
from jax.sharding import PartitionSpec as P

NZ = 8
CHUNKS = 3
MESH = pl.DeviceIdType.MESH


def with_halo(cells, sides, width):
    for axis, dim in sides:
        count = lax.axis_size(axis)
        ends = count - 1
        head = lax.slice_in_dim(cells, 0, width, axis=dim)
        tail = lax.slice_in_dim(cells, cells.shape[dim] - width, cells.shape[dim], axis=dim)
        cells = jnp.concatenate(
            [
                lax.ppermute(tail, axis, [(i, (i + 1) % count) for i in range(ends)]),
                cells,
                lax.ppermute(head, axis, [((i + 1) % count, i) for i in range(ends)]),
            ],
            axis=dim,
        )
    return cells


def shifted_stack(padded, depth):
    extent = padded.shape[1] - 2
    plane_len = padded.shape[2]
    widened = jnp.pad(padded, ((0, 0), (0, 0), (depth + 1, depth + 1)))
    z_index = jnp.arange(plane_len, dtype=jnp.int32) % depth
    pieces = []
    for step_x in (-1, 0, 1):
        x_rows = widened[:, 1 - step_x : 1 - step_x + extent, :]
        for step_y in (-1, 0, 1):
            for step_z in (-1, 0, 1):
                offset = step_y * depth + step_z
                piece = x_rows[:, :, depth + 1 - offset : depth + 1 - offset + plane_len]
                inside = (z_index - step_z >= 0) & (z_index - step_z < depth)
                pieces.append(jnp.where(inside, piece, jnp.zeros_like(piece)))
    return jnp.stack(pieces)


def gelu_slope(values):
    return 0.5 * (1.0 + jax.scipy.special.erf(values / math.sqrt(2.0))) + values * jnp.exp(
        -0.5 * values * values
    ) / math.sqrt(2.0 * math.pi)


def finish(grad_act, pre_act, down_weight):
    values = pre_act.astype(jnp.float32)
    grad_pre = (grad_act.astype(jnp.float32) * gelu_slope(values)).astype(jnp.bfloat16)
    result = lax.dot_general(
        grad_pre, down_weight, (((2,), (2,)), ((), ())), preferred_element_type=jnp.float32
    )
    return result.astype(jnp.bfloat16)


def body_blocks(grad_out, conv_weight, pre_act, down_weight):
    padded = with_halo(grad_out, ((("space", "pair"), 1),), 1)
    stacked = shifted_stack(padded, NZ)
    partial_sum = lax.dot_general(
        stacked, conv_weight, (((0, 1), (0, 1)), ((), ())), preferred_element_type=jnp.float32
    )
    grad_act = lax.psum_scatter(
        partial_sum.astype(jnp.bfloat16), "chan", scatter_dimension=1, tiled=True
    )
    return finish(grad_act, pre_act, down_weight)


def conv_kernel(
    n, ns, nx, ny, s_ref, w_ref, out_ref,
    w_all, cells, shifted, acc,
    w_send, w_recv, g_send, g_recv, h_send, h_recv, local,
):
    gy, z = lax.axis_index("groups"), lax.axis_index("chan")
    sx, core = lax.axis_index("space"), lax.axis_index("pair")
    main = NZ * ny
    chunk_rows = w_all.shape[1] // CHUNKS
    piece_rows = chunk_rows // 8
    units = CHUNKS * (n - 1)
    to_x = {"space": sx + 1 - 2 * lax.rem(sx, 2)}
    to_y = {"groups": 1 - gy}
    to_core = {"pair": 1 - core}
    cross_space = sx + 2 * core - 1
    to_cross = {"space": cross_space, "pair": 1 - core}
    has_cross = (cross_space >= 0) & (cross_space < ns)
    q = gy * 4 + lax.rem(sx, 2) * 2 + core

    def flip(gy_flip, x_flip, core_flip):
        g = 1 - gy if gy_flip else gy
        x = 1 - lax.rem(sx, 2) if x_flip else lax.rem(sx, 2)
        c = 1 - core if core_flip else core
        return g * 4 + x * 2 + c

    q_x, q_y, q_d = flip(0, 1, 0), flip(1, 0, 0), flip(1, 1, 0)
    pieces = (q, q_x, q_y, q_d)
    partner_pieces = (flip(0, 0, 1), flip(0, 1, 1), flip(1, 0, 1), flip(1, 1, 1))

    barrier = pltpu.get_barrier_semaphore()
    for hop in range(1, n):
        pl.semaphore_signal(
            barrier, inc=1, device_id={"chan": lax.rem(z + hop, n)}, device_id_type=MESH
        )
    for target in (to_x, to_y, to_core):
        pl.semaphore_signal(barrier, inc=1, device_id=target, device_id_type=MESH)

    @pl.when(has_cross)
    def _():
        pl.semaphore_signal(barrier, inc=1, device_id=to_cross, device_id_type=MESH)

    own_w = pltpu.make_async_copy(w_ref, w_all.at[z], local.at[0])
    own_g = pltpu.make_async_copy(s_ref.at[z], cells.at[z, pl.ds(1, nx)], local.at[1])
    own_w.start()
    own_g.start()

    @pl.when(has_cross)
    def _():
        pl.semaphore_wait(barrier, n + 3)

    @pl.when(jnp.logical_not(has_cross))
    def _():
        pl.semaphore_wait(barrier, n + 2)

    def w_rows(chunk, piece):
        first = chunk * chunk_rows + piece * piece_rows
        return pl.ds(pl.multiple_of(first, piece_rows), piece_rows)

    def w_copy(kind, way, step, chunk, shard, piece, target):
        view = w_all.at[shard, w_rows(chunk, piece)]
        return pltpu.make_async_remote_copy(
            src_ref=view, dst_ref=view,
            send_sem=w_send.at[kind, way, step, chunk],
            recv_sem=w_recv.at[kind, way, step, chunk],
            device_id=target, device_id_type=MESH,
        )

    def own_z_copy(way, chunk):
        return pltpu.make_async_remote_copy(
            src_ref=w_ref.at[w_rows(chunk, q)], dst_ref=w_all.at[z, w_rows(chunk, q)],
            send_sem=w_send.at[0, way, 1, chunk], recv_sem=w_recv.at[0, way, 1, chunk],
            device_id={"chan": z + 1 - 2 * way}, device_id_type=MESH,
        )

    def g_copy(way, step):
        target = z + step * (1 - 2 * way)
        return pltpu.make_async_remote_copy(
            src_ref=s_ref.at[target], dst_ref=cells.at[z, pl.ds(1, nx)],
            send_sem=g_send.at[way, step], recv_sem=g_recv.at[way, step],
            device_id={"chan": target}, device_id_type=MESH,
        )

    def g_arrival(way, step):
        shard = z - step * (1 - 2 * way)
        return pltpu.make_async_remote_copy(
            src_ref=s_ref.at[z], dst_ref=cells.at[shard, pl.ds(1, nx)],
            send_sem=g_send.at[way, step], recv_sem=g_recv.at[way, step],
            device_id={"chan": shard}, device_id_type=MESH,
        )

    def h_copy(side, way, step, shard, sending):
        last = nx + 1
        if side == 0:
            source, landing, target = nx - (nx - 1) * core, last * core, to_core
            arriving = last * (1 - core)
        else:
            source, landing, target = 1 + (nx - 1) * core, last * (1 - core), to_cross
            arriving = last * core
        return pltpu.make_async_remote_copy(
            src_ref=cells.at[shard, source],
            dst_ref=cells.at[shard, landing if sending else arriving],
            send_sem=h_send.at[side, way, step], recv_sem=h_recv.at[side, way, step],
            device_id=target, device_id_type=MESH,
        )

    def sends_on(way, step):
        return z + step < n if way == 0 else z - step >= 0

    def arrives(way, step):
        return z - step >= 0 if way == 0 else z + step < n

    def shard_of(way, step):
        return z - step if way == 0 else z + step

    def each_arrival(step, act):
        for way in (0, 1):
            @pl.when(arrives(way, step))
            def _():
                act(way, step, shard_of(way, step))

    for chunk in range(CHUNKS):
        for way in (0, 1):
            @pl.when(sends_on(way, 1))
            def _():
                own_z_copy(way, chunk).start()

    acc[...] = jnp.zeros_like(acc)

    def start_halo(way, step, shard):
        h_copy(0, way, step, shard, True).start()

        @pl.when(has_cross)
        def _():
            h_copy(1, way, step, shard, True).start()

        @pl.when(jnp.logical_not(has_cross))
        def _():
            cells[shard, (nx + 1) * core] = jnp.zeros(cells.shape[2:], cells.dtype)

    def end_halo(way, step, shard):
        h_copy(0, way, step, shard, False).wait_recv()

        @pl.when(has_cross)
        def _():
            h_copy(1, way, step, shard, False).wait_recv()

        def plane(x, carry):
            values = cells[shard, x, pl.ds(0, main)]
            edge = cells[shard, x, pl.ds(main, 2 * NZ)].astype(jnp.float32)
            wide = values.astype(jnp.float32)
            width = wide.shape[1]
            row = lax.broadcasted_iota(jnp.int32, (main, width), 0) % ny
            low = jnp.broadcast_to(edge[:NZ][:, None, :], (NZ, ny, width)).reshape(main, width)
            high = jnp.broadcast_to(edge[NZ:][:, None, :], (NZ, ny, width)).reshape(main, width)
            after = jnp.where(row == ny - 1, high, pltpu.roll(wide, main - 1, 0))
            before = jnp.where(row == 0, low, pltpu.roll(wide, 1, 0))
            shifted[0, shard, x, pl.ds(ny, main)] = after.astype(jnp.bfloat16)
            shifted[1, shard, x, pl.ds(ny, main)] = values
            shifted[2, shard, x, pl.ds(ny, main)] = before.astype(jnp.bfloat16)
            blank = jnp.zeros((ny, width), jnp.bfloat16)
            for kind in range(3):
                shifted[kind, shard, x, pl.ds(0, ny)] = blank
                shifted[kind, shard, x, pl.ds(ny + main, ny)] = blank
            return carry

        lax.fori_loop(0, nx + 2, plane, 0)

    def stage_a(way, step, chunk, shard):
        w_copy(0, way, step, chunk, shard, q, to_core).wait_recv()
        w_copy(5, way, step, chunk, shard, q, to_x).start()
        w_copy(6, way, step, chunk, shard, q, to_y).start()

        @pl.when((step < n - 1) & sends_on(way, 1))
        def _():
            w_copy(0, way, step + 1, chunk, shard, q, {"chan": z + 1 - 2 * way}).start()

        w_copy(1, way, step, chunk, shard, q, to_core).start()

    def stage_b(way, step, chunk, shard):
        w_copy(5, way, step, chunk, shard, q_x, to_x).wait_recv()

        @pl.when(core == 0)
        def _():
            w_copy(7, way, step, chunk, shard, q_x, to_y).start()

        w_copy(2, way, step, chunk, shard, q_x, to_core).start()
        w_copy(6, way, step, chunk, shard, q_y, to_y).wait_recv()

        @pl.when(core == 1)
        def _():
            w_copy(7, way, step, chunk, shard, q_y, to_x).start()

        w_copy(3, way, step, chunk, shard, q_y, to_core).start()

    def stage_c(way, step, chunk, shard):
        w_copy(7, way, step, chunk, shard, q_d, to_y).wait_recv()
        w_copy(4, way, step, chunk, shard, q_d, to_core).start()

    def multiply(shard, chunk):
        width = cells.shape[3]

        def planes(half, carry):
            parts = []
            for step_y in (-1, 0, 1):
                for step_z in (-1, 0, 1):
                    part = shifted[
                        step_y + 1, shard, pl.ds(half * 2 + 2 - chunk, 2),
                        pl.ds((1 - step_z) * ny, main),
                    ]
                    parts.append(part.reshape(2 * main, width))
            taps = w_all[shard, pl.ds(pl.multiple_of(chunk * chunk_rows, chunk_rows), chunk_rows)]
            product = jnp.dot(
                jnp.concatenate(parts, axis=1), taps, preferred_element_type=jnp.float32
            )
            acc[pl.ds(half * 2, 2)] += product.reshape(2, main, out_ref.shape[2])
            return carry

        lax.fori_loop(0, nx // 2, planes, 0)

    def compute(way, step, chunk, shard):
        @pl.when(chunk == 0)
        def _():
            end_halo(way, step, shard)

        for kind in range(4):
            w_copy(
                1 + kind, way, step, chunk, shard, partner_pieces[kind], to_core
            ).wait_recv()
        multiply(shard, chunk)

    def run(unit, stage):
        step, chunk = 1 + unit // CHUNKS, unit % CHUNKS
        each_arrival(step, lambda way, step, shard: stage(way, step, chunk, shard))

    def g_arrived(way, step, shard):
        g_arrival(way, step).wait_recv()
        start_halo(way, step, shard)

    own_g.wait()
    start_halo(0, 0, z)
    own_w.wait()
    end_halo(0, 0, z)

    def turn(k, carry):
        @pl.when(k < units)
        def _():
            run(k, stage_a)

        @pl.when((k % 2 == 0) & (k // 2 + 1 < n))
        def _():
            step = k // 2 + 1
            for way in (0, 1):
                @pl.when(sends_on(way, step))
                def _():
                    g_copy(way, step).start()

        @pl.when((k >= 1) & (k < units + 1))
        def _():
            run(k - 1, stage_b)

        @pl.when((k >= 2) & (k < units + 2))
        def _():
            run(k - 2, stage_c)

        @pl.when((k < units) & (k % CHUNKS == CHUNKS - 1))
        def _():
            each_arrival(1 + k // CHUNKS, g_arrived)

        @pl.when(k < CHUNKS)
        def _():
            multiply(z, k)

        @pl.when(k >= 3)
        def _():
            run(k - 3, compute)

        return carry

    lax.fori_loop(0, units + 3, turn, 0)
    out_ref[...] = acc[...].astype(out_ref.dtype)

    def end_sends(way, step, chunk, shard):
        w_copy(5, way, step, chunk, shard, q, to_x).wait_send()
        w_copy(6, way, step, chunk, shard, q, to_y).wait_send()
        for kind in range(4):
            w_copy(1 + kind, way, step, chunk, shard, pieces[kind], to_core).wait_send()

        @pl.when(core == 0)
        def _():
            w_copy(7, way, step, chunk, shard, q_x, to_y).wait_send()

        @pl.when(core == 1)
        def _():
            w_copy(7, way, step, chunk, shard, q_y, to_x).wait_send()

        @pl.when((step < n - 1) & sends_on(way, 1))
        def _():
            w_copy(0, way, step + 1, chunk, shard, q, {"chan": z + 1 - 2 * way}).wait_send()

        @pl.when(chunk == 0)
        def _():
            end_halo_sends(way, step, shard)

    def end_halo_sends(way, step, shard):
        h_copy(0, way, step, shard, True).wait_send()

        @pl.when(has_cross)
        def _():
            h_copy(1, way, step, shard, True).wait_send()

    end_halo_sends(0, 0, z)

    def close(unit, carry):
        run(unit, end_sends)
        return carry

    lax.fori_loop(0, units, close, 0)
    for way in (0, 1):
        @pl.when(sends_on(way, 1))
        def _():
            for chunk in range(CHUNKS):
                own_z_copy(way, chunk).wait_send()
        for step in range(1, n):
            @pl.when(sends_on(way, step))
            def _():
                g_copy(way, step).wait_send()


def body_gather(n, ns, grad_out, conv_weight, pre_act, down_weight):
    channels, nx, plane = grad_out.shape
    rows_y = plane // NZ
    ny = rows_y // n
    wide = conv_weight.shape[2]
    main = NZ * ny
    turned = grad_out.reshape(channels, nx, rows_y, NZ).transpose(1, 3, 2, 0)
    edged = jnp.pad(turned, ((0, 0), (0, 0), (1, 1), (0, 0)))
    blocks = turned.reshape(nx, NZ, n, ny, channels).transpose(2, 0, 1, 3, 4)
    blocks = blocks.reshape(n, nx, main, channels)
    low = edged[:, :, 0 : rows_y : ny].transpose(2, 0, 1, 3)
    high = edged[:, :, ny + 1 :: ny].transpose(2, 0, 1, 3)
    send = jnp.concatenate([blocks, low, high], axis=2)
    weights = conv_weight.reshape(-1, wide)
    vmem = pltpu.VMEM
    dma = pltpu.SemaphoreType.DMA
    grad_act = pl.pallas_call(
        functools.partial(conv_kernel, n, ns, nx, ny),
        out_shape=jax.ShapeDtypeStruct((nx, main, wide), jnp.bfloat16),
        in_specs=[pl.BlockSpec(memory_space=pl.ANY)] * 2,
        out_specs=pl.BlockSpec(memory_space=pltpu.VMEM),
        scratch_shapes=[
            vmem((n, weights.shape[0], wide), jnp.bfloat16),
            vmem((n, nx + 2, main + 2 * NZ, channels), jnp.bfloat16),
            vmem((3, n, nx + 2, main + 2 * ny, channels), jnp.bfloat16),
            vmem((nx, main, wide), jnp.float32),
            dma((8, 2, n, CHUNKS)), dma((8, 2, n, CHUNKS)),
            dma((2, n)), dma((2, n)),
            dma((2, 2, n)), dma((2, 2, n)),
            dma((2,)),
        ],
        compiler_params=pltpu.CompilerParams(
            collective_id=0, has_side_effects=True, vmem_limit_bytes=56 * 2**20
        ),
        cost_estimate=pl.CostEstimate(
            flops=2 * 27 * n * channels * nx * main * wide,
            bytes_accessed=8 * 2**20, transcendentals=0,
        ),
    )(send, weights)
    grad_act = grad_act.reshape(nx, NZ, ny, wide).transpose(0, 2, 1, 3).reshape(nx, main, wide)
    return finish(grad_act, pre_act, down_weight)


def solution(mesh):
    in_specs = (
        P("chan", ("groups", "space", "pair"), None),
        P(None, "chan", None),
        P(("groups", "space", "pair"), "chan", None),
        P(),
    )
    out_specs = P(("groups", "space", "pair"), "chan", None, None)
    n, ns = mesh.shape["chan"], mesh.shape["space"]

    def body(grad_out, conv_weight, pre_act, down_weight):
        channels, nx, plane = grad_out.shape
        ny = plane // NZ // n
        fits = channels % 128 == 0 and ny % 16 == 0 and nx % 2 == 0 and ns % 2 == 0
        fits = fits and mesh.shape["groups"] == 2 and mesh.shape["pair"] == 2
        if fits:
            return body_gather(n, ns, grad_out, conv_weight, pre_act, down_weight)
        return body_blocks(grad_out, conv_weight, pre_act, down_weight)

    return jax.shard_map(body, mesh=mesh, in_specs=in_specs, out_specs=out_specs, check_vma=False)
```

```python
import functools
import math

import jax
import jax.numpy as jnp
from jax import lax
from jax.experimental import pallas as pl
from jax.experimental.pallas import tpu as pltpu
from jax.sharding import PartitionSpec as P

NZ = 8
CHUNKS = 3
MESH = pl.DeviceIdType.MESH


def with_halo(cells, sides, width):
    for axis, dim in sides:
        count = lax.axis_size(axis)
        ends = count - 1
        head = lax.slice_in_dim(cells, 0, width, axis=dim)
        tail = lax.slice_in_dim(cells, cells.shape[dim] - width, cells.shape[dim], axis=dim)
        cells = jnp.concatenate(
            [
                lax.ppermute(tail, axis, [(i, (i + 1) % count) for i in range(ends)]),
                cells,
                lax.ppermute(head, axis, [((i + 1) % count, i) for i in range(ends)]),
            ],
            axis=dim,
        )
    return cells


def shifted_stack(padded, depth):
    extent = padded.shape[1] - 2
    plane_len = padded.shape[2]
    widened = jnp.pad(padded, ((0, 0), (0, 0), (depth + 1, depth + 1)))
    z_index = jnp.arange(plane_len, dtype=jnp.int32) % depth
    pieces = []
    for step_x in (-1, 0, 1):
        x_rows = widened[:, 1 - step_x : 1 - step_x + extent, :]
        for step_y in (-1, 0, 1):
            for step_z in (-1, 0, 1):
                offset = step_y * depth + step_z
                piece = x_rows[:, :, depth + 1 - offset : depth + 1 - offset + plane_len]
                inside = (z_index - step_z >= 0) & (z_index - step_z < depth)
                pieces.append(jnp.where(inside, piece, jnp.zeros_like(piece)))
    return jnp.stack(pieces)


def gelu_slope(values):
    return 0.5 * (1.0 + jax.scipy.special.erf(values / math.sqrt(2.0))) + values * jnp.exp(
        -0.5 * values * values
    ) / math.sqrt(2.0 * math.pi)


def finish(grad_act, pre_act, down_weight):
    values = pre_act.astype(jnp.float32)
    grad_pre = (grad_act.astype(jnp.float32) * gelu_slope(values)).astype(jnp.bfloat16)
    result = lax.dot_general(
        grad_pre, down_weight, (((2,), (2,)), ((), ())), preferred_element_type=jnp.float32
    )
    return result.astype(jnp.bfloat16)


def body_blocks(grad_out, conv_weight, pre_act, down_weight):
    padded = with_halo(grad_out, ((("space", "pair"), 1),), 1)
    stacked = shifted_stack(padded, NZ)
    partial_sum = lax.dot_general(
        stacked, conv_weight, (((0, 1), (0, 1)), ((), ())), preferred_element_type=jnp.float32
    )
    grad_act = lax.psum_scatter(
        partial_sum.astype(jnp.bfloat16), "chan", scatter_dimension=1, tiled=True
    )
    return finish(grad_act, pre_act, down_weight)


def conv_kernel(
    n, ns, nx, ny, s_ref, w_ref, out_ref,
    w_all, cells, shifted, acc,
    w_send, w_recv, g_send, g_recv, h_send, h_recv, local,
):
    gy, z = lax.axis_index("groups"), lax.axis_index("chan")
    sx, core = lax.axis_index("space"), lax.axis_index("pair")
    main = NZ * ny
    chunk_rows = w_all.shape[1] // CHUNKS
    piece_rows = chunk_rows // 8
    units = CHUNKS * (n - 1)
    to_x = {"space": sx + 1 - 2 * lax.rem(sx, 2)}
    to_y = {"groups": 1 - gy}
    to_core = {"pair": 1 - core}
    cross_space = sx + 2 * core - 1
    to_cross = {"space": cross_space, "pair": 1 - core}
    has_cross = (cross_space >= 0) & (cross_space < ns)
    q = gy * 4 + lax.rem(sx, 2) * 2 + core

    def flip(gy_flip, x_flip, core_flip):
        g = 1 - gy if gy_flip else gy
        x = 1 - lax.rem(sx, 2) if x_flip else lax.rem(sx, 2)
        c = 1 - core if core_flip else core
        return g * 4 + x * 2 + c

    q_x, q_y, q_d = flip(0, 1, 0), flip(1, 0, 0), flip(1, 1, 0)
    pieces = (q, q_x, q_y, q_d)
    partner_pieces = (flip(0, 0, 1), flip(0, 1, 1), flip(1, 0, 1), flip(1, 1, 1))

    barrier = pltpu.get_barrier_semaphore()
    for hop in range(1, n):
        pl.semaphore_signal(
            barrier, inc=1, device_id={"chan": lax.rem(z + hop, n)}, device_id_type=MESH
        )
    for target in (to_x, to_y, to_core):
        pl.semaphore_signal(barrier, inc=1, device_id=target, device_id_type=MESH)

    @pl.when(has_cross)
    def _():
        pl.semaphore_signal(barrier, inc=1, device_id=to_cross, device_id_type=MESH)

    own_w = pltpu.make_async_copy(w_ref, w_all.at[z], local.at[0])
    own_g = pltpu.make_async_copy(s_ref.at[z], cells.at[z, pl.ds(1, nx)], local.at[1])
    own_w.start()
    own_g.start()

    @pl.when(has_cross)
    def _():
        pl.semaphore_wait(barrier, n + 3)

    @pl.when(jnp.logical_not(has_cross))
    def _():
        pl.semaphore_wait(barrier, n + 2)

    def w_rows(chunk, piece):
        first = chunk * chunk_rows + piece * piece_rows
        return pl.ds(pl.multiple_of(first, piece_rows), piece_rows)

    def w_copy(kind, way, step, chunk, shard, piece, target):
        view = w_all.at[shard, w_rows(chunk, piece)]
        return pltpu.make_async_remote_copy(
            src_ref=view, dst_ref=view,
            send_sem=w_send.at[kind, way, step, chunk],
            recv_sem=w_recv.at[kind, way, step, chunk],
            device_id=target, device_id_type=MESH,
        )

    def own_z_copy(way, chunk):
        return pltpu.make_async_remote_copy(
            src_ref=w_ref.at[w_rows(chunk, q)], dst_ref=w_all.at[z, w_rows(chunk, q)],
            send_sem=w_send.at[0, way, 1, chunk], recv_sem=w_recv.at[0, way, 1, chunk],
            device_id={"chan": z + 1 - 2 * way}, device_id_type=MESH,
        )

    def g_copy(way, step):
        target = z + step * (1 - 2 * way)
        return pltpu.make_async_remote_copy(
            src_ref=s_ref.at[target], dst_ref=cells.at[z, pl.ds(1, nx)],
            send_sem=g_send.at[way, step], recv_sem=g_recv.at[way, step],
            device_id={"chan": target}, device_id_type=MESH,
        )

    def g_arrival(way, step):
        shard = z - step * (1 - 2 * way)
        return pltpu.make_async_remote_copy(
            src_ref=s_ref.at[z], dst_ref=cells.at[shard, pl.ds(1, nx)],
            send_sem=g_send.at[way, step], recv_sem=g_recv.at[way, step],
            device_id={"chan": shard}, device_id_type=MESH,
        )

    def h_copy(side, way, step, shard, sending):
        last = nx + 1
        if side == 0:
            source, landing, target = nx - (nx - 1) * core, last * core, to_core
            arriving = last * (1 - core)
        else:
            source, landing, target = 1 + (nx - 1) * core, last * (1 - core), to_cross
            arriving = last * core
        return pltpu.make_async_remote_copy(
            src_ref=cells.at[shard, source],
            dst_ref=cells.at[shard, landing if sending else arriving],
            send_sem=h_send.at[side, way, step], recv_sem=h_recv.at[side, way, step],
            device_id=target, device_id_type=MESH,
        )

    def sends_on(way, step):
        return z + step < n if way == 0 else z - step >= 0

    def arrives(way, step):
        return z - step >= 0 if way == 0 else z + step < n

    def shard_of(way, step):
        return z - step if way == 0 else z + step

    def each_arrival(step, act):
        for way in (0, 1):
            @pl.when(arrives(way, step))
            def _():
                act(way, step, shard_of(way, step))

    for chunk in range(CHUNKS):
        for way in (0, 1):
            @pl.when(sends_on(way, 1))
            def _():
                own_z_copy(way, chunk).start()

    acc[...] = jnp.zeros_like(acc)

    def start_halo(way, step, shard):
        h_copy(0, way, step, shard, True).start()

        @pl.when(has_cross)
        def _():
            h_copy(1, way, step, shard, True).start()

        @pl.when(jnp.logical_not(has_cross))
        def _():
            cells[shard, (nx + 1) * core] = jnp.zeros(cells.shape[2:], cells.dtype)

    def end_halo(way, step, shard):
        h_copy(0, way, step, shard, False).wait_recv()

        @pl.when(has_cross)
        def _():
            h_copy(1, way, step, shard, False).wait_recv()

        def plane(x, carry):
            values = cells[shard, x, pl.ds(0, main)]
            edge = cells[shard, x, pl.ds(main, 2 * NZ)].astype(jnp.float32)
            wide = values.astype(jnp.float32)
            width = wide.shape[1]
            row = lax.broadcasted_iota(jnp.int32, (main, width), 0) % ny
            low = jnp.broadcast_to(edge[:NZ][:, None, :], (NZ, ny, width)).reshape(main, width)
            high = jnp.broadcast_to(edge[NZ:][:, None, :], (NZ, ny, width)).reshape(main, width)
            after = jnp.where(row == ny - 1, high, pltpu.roll(wide, main - 1, 0))
            before = jnp.where(row == 0, low, pltpu.roll(wide, 1, 0))
            shifted[0, shard, x, pl.ds(ny, main)] = after.astype(jnp.bfloat16)
            shifted[1, shard, x, pl.ds(ny, main)] = values
            shifted[2, shard, x, pl.ds(ny, main)] = before.astype(jnp.bfloat16)
            blank = jnp.zeros((ny, width), jnp.bfloat16)
            for kind in range(3):
                shifted[kind, shard, x, pl.ds(0, ny)] = blank
                shifted[kind, shard, x, pl.ds(ny + main, ny)] = blank
            return carry

        lax.fori_loop(0, nx + 2, plane, 0)

    def stage_z(way, step, chunk, shard):
        @pl.when(sends_on(way, 1))
        def _():
            w_copy(0, way, step, chunk, shard, q, to_core).wait_recv()
            w_copy(0, way, step + 1, chunk, shard, q, {"chan": z + 1 - 2 * way}).start()

    def stage_a(way, step, chunk, shard):
        @pl.when(jnp.logical_not(sends_on(way, 1)))
        def _():
            w_copy(0, way, step, chunk, shard, q, to_core).wait_recv()

        w_copy(5, way, step, chunk, shard, q, to_x).start()
        w_copy(6, way, step, chunk, shard, q, to_y).start()
        w_copy(1, way, step, chunk, shard, q, to_core).start()

    def stage_b(way, step, chunk, shard):
        w_copy(5, way, step, chunk, shard, q_x, to_x).wait_recv()

        @pl.when(core == 0)
        def _():
            w_copy(7, way, step, chunk, shard, q_x, to_y).start()

        w_copy(2, way, step, chunk, shard, q_x, to_core).start()
        w_copy(6, way, step, chunk, shard, q_y, to_y).wait_recv()

        @pl.when(core == 1)
        def _():
            w_copy(7, way, step, chunk, shard, q_y, to_x).start()

        w_copy(3, way, step, chunk, shard, q_y, to_core).start()

    def stage_c(way, step, chunk, shard):
        w_copy(7, way, step, chunk, shard, q_d, to_y).wait_recv()
        w_copy(4, way, step, chunk, shard, q_d, to_core).start()

    def multiply(shard, chunk):
        width = cells.shape[3]

        def planes(half, carry):
            parts = []
            for step_y in (-1, 0, 1):
                for step_z in (-1, 0, 1):
                    part = shifted[
                        step_y + 1, shard, pl.ds(half * 2 + 2 - chunk, 2),
                        pl.ds((1 - step_z) * ny, main),
                    ]
                    parts.append(part.reshape(2 * main, width))
            taps = w_all[shard, pl.ds(pl.multiple_of(chunk * chunk_rows, chunk_rows), chunk_rows)]
            product = jnp.dot(
                jnp.concatenate(parts, axis=1), taps, preferred_element_type=jnp.float32
            )
            acc[pl.ds(half * 2, 2)] += product.reshape(2, main, out_ref.shape[2])
            return carry

        lax.fori_loop(0, nx // 2, planes, 0)

    def compute(way, step, chunk, shard):
        @pl.when(chunk == 0)
        def _():
            end_halo(way, step, shard)

        for kind in range(4):
            w_copy(
                1 + kind, way, step, chunk, shard, partner_pieces[kind], to_core
            ).wait_recv()
        multiply(shard, chunk)

    def run(unit, stage):
        step, chunk = 1 + unit // CHUNKS, unit % CHUNKS
        each_arrival(step, lambda way, step, shard: stage(way, step, chunk, shard))

    def g_arrived(way, step, shard):
        g_arrival(way, step).wait_recv()
        start_halo(way, step, shard)

    own_g.wait()
    start_halo(0, 0, z)
    own_w.wait()
    end_halo(0, 0, z)

    def turn(k, carry):
        @pl.when((k >= 1) & (2 * k - 1 < units))
        def _():
            run(2 * k - 1, stage_z)

        @pl.when(2 * k < units)
        def _():
            run(2 * k, stage_z)

        @pl.when(k < units)
        def _():
            run(k, stage_a)

        @pl.when(k + 1 < n)
        def _():
            step = k + 1
            for way in (0, 1):
                @pl.when(sends_on(way, step))
                def _():
                    g_copy(way, step).start()

        @pl.when((k >= 1) & (k < units + 1))
        def _():
            run(k - 1, stage_b)

        @pl.when((k >= 2) & (k < units + 2))
        def _():
            run(k - 2, stage_c)

        @pl.when((k < units) & (k % CHUNKS == CHUNKS - 1))
        def _():
            each_arrival(1 + k // CHUNKS, g_arrived)

        @pl.when(k < CHUNKS)
        def _():
            multiply(z, k)

        @pl.when(k >= 3)
        def _():
            run(k - 3, compute)

        return carry

    lax.fori_loop(0, units + 3, turn, 0)
    out_ref[...] = acc[...].astype(out_ref.dtype)

    def end_sends(way, step, chunk, shard):
        w_copy(5, way, step, chunk, shard, q, to_x).wait_send()
        w_copy(6, way, step, chunk, shard, q, to_y).wait_send()
        for kind in range(4):
            w_copy(1 + kind, way, step, chunk, shard, pieces[kind], to_core).wait_send()

        @pl.when(core == 0)
        def _():
            w_copy(7, way, step, chunk, shard, q_x, to_y).wait_send()

        @pl.when(core == 1)
        def _():
            w_copy(7, way, step, chunk, shard, q_y, to_x).wait_send()

        @pl.when(sends_on(way, 1))
        def _():
            w_copy(0, way, step + 1, chunk, shard, q, {"chan": z + 1 - 2 * way}).wait_send()

        @pl.when(chunk == 0)
        def _():
            end_halo_sends(way, step, shard)

    def end_halo_sends(way, step, shard):
        h_copy(0, way, step, shard, True).wait_send()

        @pl.when(has_cross)
        def _():
            h_copy(1, way, step, shard, True).wait_send()

    end_halo_sends(0, 0, z)

    def close(unit, carry):
        run(unit, end_sends)
        return carry

    lax.fori_loop(0, units, close, 0)
    for way in (0, 1):
        @pl.when(sends_on(way, 1))
        def _():
            for chunk in range(CHUNKS):
                own_z_copy(way, chunk).wait_send()
        for step in range(1, n):
            @pl.when(sends_on(way, step))
            def _():
                g_copy(way, step).wait_send()


def body_gather(n, ns, grad_out, conv_weight, pre_act, down_weight):
    channels, nx, plane = grad_out.shape
    rows_y = plane // NZ
    ny = rows_y // n
    wide = conv_weight.shape[2]
    main = NZ * ny
    turned = grad_out.reshape(channels, nx, rows_y, NZ).transpose(1, 3, 2, 0)
    edged = jnp.pad(turned, ((0, 0), (0, 0), (1, 1), (0, 0)))
    blocks = turned.reshape(nx, NZ, n, ny, channels).transpose(2, 0, 1, 3, 4)
    blocks = blocks.reshape(n, nx, main, channels)
    low = edged[:, :, 0 : rows_y : ny].transpose(2, 0, 1, 3)
    high = edged[:, :, ny + 1 :: ny].transpose(2, 0, 1, 3)
    send = jnp.concatenate([blocks, low, high], axis=2)
    weights = conv_weight.reshape(-1, wide)
    vmem = pltpu.VMEM
    dma = pltpu.SemaphoreType.DMA
    grad_act = pl.pallas_call(
        functools.partial(conv_kernel, n, ns, nx, ny),
        out_shape=jax.ShapeDtypeStruct((nx, main, wide), jnp.bfloat16),
        in_specs=[pl.BlockSpec(memory_space=pl.ANY)] * 2,
        out_specs=pl.BlockSpec(memory_space=pltpu.VMEM),
        scratch_shapes=[
            vmem((n, weights.shape[0], wide), jnp.bfloat16),
            vmem((n, nx + 2, main + 2 * NZ, channels), jnp.bfloat16),
            vmem((3, n, nx + 2, main + 2 * ny, channels), jnp.bfloat16),
            vmem((nx, main, wide), jnp.float32),
            dma((8, 2, n, CHUNKS)), dma((8, 2, n, CHUNKS)),
            dma((2, n)), dma((2, n)),
            dma((2, 2, n)), dma((2, 2, n)),
            dma((2,)),
        ],
        compiler_params=pltpu.CompilerParams(
            collective_id=0, has_side_effects=True, vmem_limit_bytes=56 * 2**20
        ),
        cost_estimate=pl.CostEstimate(
            flops=2 * 27 * n * channels * nx * main * wide,
            bytes_accessed=8 * 2**20, transcendentals=0,
        ),
    )(send, weights)
    grad_act = grad_act.reshape(nx, NZ, ny, wide).transpose(0, 2, 1, 3).reshape(nx, main, wide)
    return finish(grad_act, pre_act, down_weight)


def solution(mesh):
    in_specs = (
        P("chan", ("groups", "space", "pair"), None),
        P(None, "chan", None),
        P(("groups", "space", "pair"), "chan", None),
        P(),
    )
    out_specs = P(("groups", "space", "pair"), "chan", None, None)
    n, ns = mesh.shape["chan"], mesh.shape["space"]

    def body(grad_out, conv_weight, pre_act, down_weight):
        channels, nx, plane = grad_out.shape
        ny = plane // NZ // n
        fits = channels % 128 == 0 and ny % 16 == 0 and nx % 2 == 0 and ns % 2 == 0
        fits = fits and mesh.shape["groups"] == 2 and mesh.shape["pair"] == 2
        if fits:
            return body_gather(n, ns, grad_out, conv_weight, pre_act, down_weight)
        return body_blocks(grad_out, conv_weight, pre_act, down_weight)

    return jax.shard_map(body, mesh=mesh, in_specs=in_specs, out_specs=out_specs, check_vma=False)
```

```python
import functools
import math

import jax
import jax.numpy as jnp
from jax import lax
from jax.experimental import pallas as pl
from jax.experimental.pallas import tpu as pltpu
from jax.sharding import PartitionSpec as P

NZ = 8
CHUNKS = 3
MESH = pl.DeviceIdType.MESH


def with_halo(cells, sides, width):
    for axis, dim in sides:
        count = lax.axis_size(axis)
        ends = count - 1
        head = lax.slice_in_dim(cells, 0, width, axis=dim)
        tail = lax.slice_in_dim(cells, cells.shape[dim] - width, cells.shape[dim], axis=dim)
        cells = jnp.concatenate(
            [
                lax.ppermute(tail, axis, [(i, (i + 1) % count) for i in range(ends)]),
                cells,
                lax.ppermute(head, axis, [((i + 1) % count, i) for i in range(ends)]),
            ],
            axis=dim,
        )
    return cells


def shifted_stack(padded, depth):
    extent = padded.shape[1] - 2
    plane_len = padded.shape[2]
    widened = jnp.pad(padded, ((0, 0), (0, 0), (depth + 1, depth + 1)))
    z_index = jnp.arange(plane_len, dtype=jnp.int32) % depth
    pieces = []
    for step_x in (-1, 0, 1):
        x_rows = widened[:, 1 - step_x : 1 - step_x + extent, :]
        for step_y in (-1, 0, 1):
            for step_z in (-1, 0, 1):
                offset = step_y * depth + step_z
                piece = x_rows[:, :, depth + 1 - offset : depth + 1 - offset + plane_len]
                inside = (z_index - step_z >= 0) & (z_index - step_z < depth)
                pieces.append(jnp.where(inside, piece, jnp.zeros_like(piece)))
    return jnp.stack(pieces)


def gelu_slope(values):
    return 0.5 * (1.0 + jax.scipy.special.erf(values / math.sqrt(2.0))) + values * jnp.exp(
        -0.5 * values * values
    ) / math.sqrt(2.0 * math.pi)


def finish(grad_act, pre_act, down_weight):
    values = pre_act.astype(jnp.float32)
    grad_pre = (grad_act.astype(jnp.float32) * gelu_slope(values)).astype(jnp.bfloat16)
    result = lax.dot_general(
        grad_pre, down_weight, (((2,), (2,)), ((), ())), preferred_element_type=jnp.float32
    )
    return result.astype(jnp.bfloat16)


def down_kernel(taps, grad_ref, weight_ref, out_ref, total):
    rows = grad_ref.shape[1]
    for tap in range(taps):
        part = lax.dot_general(
            grad_ref[0], weight_ref[tap], (((1,), (1,)), ((), ())),
            preferred_element_type=jnp.float32,
        )
        for lanes in range(0, part.shape[1], 128):
            total[lanes // 128, pl.ds(tap, rows, stride=taps), :] = part[:, lanes : lanes + 128]
    for half in range(total.shape[0]):
        out_ref[0, :, half * 128 : half * 128 + 128] = total[half].astype(out_ref.dtype)


def finish_planes(grad_act, pre_act, down_weight):
    values = pre_act.astype(jnp.float32)
    grad_pre = (grad_act.astype(jnp.float32) * gelu_slope(values)).astype(jnp.bfloat16)
    nx, rows, channels = grad_pre.shape
    taps, fine, _ = down_weight.shape
    result = pl.pallas_call(
        functools.partial(down_kernel, taps),
        grid=(nx,),
        out_shape=jax.ShapeDtypeStruct((nx, rows * taps, fine), jnp.bfloat16),
        in_specs=[
            pl.BlockSpec((1, rows, channels), lambda i: (i, 0, 0)),
            pl.BlockSpec((taps, fine, channels), lambda i: (0, 0, 0)),
        ],
        out_specs=pl.BlockSpec((1, rows * taps, fine), lambda i: (i, 0, 0)),
        scratch_shapes=[pltpu.VMEM((fine // 128, rows * taps, 128), jnp.float32)],
        compiler_params=pltpu.CompilerParams(vmem_limit_bytes=32 * 2**20),
    )(grad_pre, down_weight)
    return result.reshape(nx, rows, taps, fine)


def body_blocks(grad_out, conv_weight, pre_act, down_weight):
    padded = with_halo(grad_out, ((("space", "pair"), 1),), 1)
    stacked = shifted_stack(padded, NZ)
    partial_sum = lax.dot_general(
        stacked, conv_weight, (((0, 1), (0, 1)), ((), ())), preferred_element_type=jnp.float32
    )
    grad_act = lax.psum_scatter(
        partial_sum.astype(jnp.bfloat16), "chan", scatter_dimension=1, tiled=True
    )
    return finish(grad_act, pre_act, down_weight)


def conv_kernel(
    n, ns, nx, ny, s_ref, w_ref, out_ref,
    w_all, cells, shifted, acc,
    w_send, w_recv, g_send, g_recv, h_send, h_recv, local,
):
    gy, z = lax.axis_index("groups"), lax.axis_index("chan")
    sx, core = lax.axis_index("space"), lax.axis_index("pair")
    main = NZ * ny
    chunk_rows = w_all.shape[1] // CHUNKS
    piece_rows = chunk_rows // 8
    units = CHUNKS * (n - 1)
    to_x = {"space": sx + 1 - 2 * lax.rem(sx, 2)}
    to_y = {"groups": 1 - gy}
    to_core = {"pair": 1 - core}
    cross_space = sx + 2 * core - 1
    to_cross = {"space": cross_space, "pair": 1 - core}
    has_cross = (cross_space >= 0) & (cross_space < ns)
    q = gy * 4 + lax.rem(sx, 2) * 2 + core

    def flip(gy_flip, x_flip, core_flip):
        g = 1 - gy if gy_flip else gy
        x = 1 - lax.rem(sx, 2) if x_flip else lax.rem(sx, 2)
        c = 1 - core if core_flip else core
        return g * 4 + x * 2 + c

    q_x, q_y, q_d = flip(0, 1, 0), flip(1, 0, 0), flip(1, 1, 0)
    pieces = (q, q_x, q_y, q_d)
    partner_pieces = (flip(0, 0, 1), flip(0, 1, 1), flip(1, 0, 1), flip(1, 1, 1))

    barrier = pltpu.get_barrier_semaphore()
    for hop in range(1, n):
        pl.semaphore_signal(
            barrier, inc=1, device_id={"chan": lax.rem(z + hop, n)}, device_id_type=MESH
        )
    for target in (to_x, to_y, to_core):
        pl.semaphore_signal(barrier, inc=1, device_id=target, device_id_type=MESH)

    @pl.when(has_cross)
    def _():
        pl.semaphore_signal(barrier, inc=1, device_id=to_cross, device_id_type=MESH)

    own_w = pltpu.make_async_copy(w_ref, w_all.at[z], local.at[0])
    own_g = pltpu.make_async_copy(s_ref.at[z], cells.at[z, pl.ds(1, nx)], local.at[1])
    own_w.start()
    own_g.start()

    @pl.when(has_cross)
    def _():
        pl.semaphore_wait(barrier, n + 3)

    @pl.when(jnp.logical_not(has_cross))
    def _():
        pl.semaphore_wait(barrier, n + 2)

    def w_rows(chunk, piece):
        first = chunk * chunk_rows + piece * piece_rows
        return pl.ds(pl.multiple_of(first, piece_rows), piece_rows)

    def w_copy(kind, way, step, chunk, shard, piece, target):
        view = w_all.at[shard, w_rows(chunk, piece)]
        return pltpu.make_async_remote_copy(
            src_ref=view, dst_ref=view,
            send_sem=w_send.at[kind, way, step, chunk],
            recv_sem=w_recv.at[kind, way, step, chunk],
            device_id=target, device_id_type=MESH,
        )

    def own_z_copy(way, chunk):
        return pltpu.make_async_remote_copy(
            src_ref=w_ref.at[w_rows(chunk, q)], dst_ref=w_all.at[z, w_rows(chunk, q)],
            send_sem=w_send.at[0, way, 1, chunk], recv_sem=w_recv.at[0, way, 1, chunk],
            device_id={"chan": z + 1 - 2 * way}, device_id_type=MESH,
        )

    def g_copy(way, step):
        target = z + step * (1 - 2 * way)
        return pltpu.make_async_remote_copy(
            src_ref=s_ref.at[target], dst_ref=cells.at[z, pl.ds(1, nx)],
            send_sem=g_send.at[way, step], recv_sem=g_recv.at[way, step],
            device_id={"chan": target}, device_id_type=MESH,
        )

    def g_arrival(way, step):
        shard = z - step * (1 - 2 * way)
        return pltpu.make_async_remote_copy(
            src_ref=s_ref.at[z], dst_ref=cells.at[shard, pl.ds(1, nx)],
            send_sem=g_send.at[way, step], recv_sem=g_recv.at[way, step],
            device_id={"chan": shard}, device_id_type=MESH,
        )

    def h_copy(side, way, step, shard, sending):
        last = nx + 1
        if side == 0:
            source, landing, target = nx - (nx - 1) * core, last * core, to_core
            arriving = last * (1 - core)
        else:
            source, landing, target = 1 + (nx - 1) * core, last * (1 - core), to_cross
            arriving = last * core
        return pltpu.make_async_remote_copy(
            src_ref=cells.at[shard, source],
            dst_ref=cells.at[shard, landing if sending else arriving],
            send_sem=h_send.at[side, way, step], recv_sem=h_recv.at[side, way, step],
            device_id=target, device_id_type=MESH,
        )

    def sends_on(way, step):
        return z + step < n if way == 0 else z - step >= 0

    def arrives(way, step):
        return z - step >= 0 if way == 0 else z + step < n

    def shard_of(way, step):
        return z - step if way == 0 else z + step

    def each_arrival(step, act):
        for way in (0, 1):
            @pl.when(arrives(way, step))
            def _():
                act(way, step, shard_of(way, step))

    for chunk in range(CHUNKS):
        for way in (0, 1):
            @pl.when(sends_on(way, 1))
            def _():
                own_z_copy(way, chunk).start()

    acc[...] = jnp.zeros_like(acc)

    def start_halo(way, step, shard):
        h_copy(0, way, step, shard, True).start()

        @pl.when(has_cross)
        def _():
            h_copy(1, way, step, shard, True).start()

        @pl.when(jnp.logical_not(has_cross))
        def _():
            cells[shard, (nx + 1) * core] = jnp.zeros(cells.shape[2:], cells.dtype)

    def end_halo(way, step, shard):
        h_copy(0, way, step, shard, False).wait_recv()

        @pl.when(has_cross)
        def _():
            h_copy(1, way, step, shard, False).wait_recv()

        def plane(x, carry):
            values = cells[shard, x, pl.ds(0, main)]
            edge = cells[shard, x, pl.ds(main, 2 * NZ)].astype(jnp.float32)
            wide = values.astype(jnp.float32)
            width = wide.shape[1]
            row = lax.broadcasted_iota(jnp.int32, (main, width), 0) % ny
            low = jnp.broadcast_to(edge[:NZ][:, None, :], (NZ, ny, width)).reshape(main, width)
            high = jnp.broadcast_to(edge[NZ:][:, None, :], (NZ, ny, width)).reshape(main, width)
            after = jnp.where(row == ny - 1, high, pltpu.roll(wide, main - 1, 0))
            before = jnp.where(row == 0, low, pltpu.roll(wide, 1, 0))
            shifted[0, shard, x, pl.ds(ny, main)] = after.astype(jnp.bfloat16)
            shifted[1, shard, x, pl.ds(ny, main)] = values
            shifted[2, shard, x, pl.ds(ny, main)] = before.astype(jnp.bfloat16)
            blank = jnp.zeros((ny, width), jnp.bfloat16)
            for kind in range(3):
                shifted[kind, shard, x, pl.ds(0, ny)] = blank
                shifted[kind, shard, x, pl.ds(ny + main, ny)] = blank
            return carry

        lax.fori_loop(0, nx + 2, plane, 0)

    def stage_a(way, step, chunk, shard):
        w_copy(0, way, step, chunk, shard, q, to_core).wait_recv()
        w_copy(5, way, step, chunk, shard, q, to_x).start()
        w_copy(6, way, step, chunk, shard, q, to_y).start()

        @pl.when((step < n - 1) & sends_on(way, 1))
        def _():
            w_copy(0, way, step + 1, chunk, shard, q, {"chan": z + 1 - 2 * way}).start()

        w_copy(1, way, step, chunk, shard, q, to_core).start()

    def stage_b(way, step, chunk, shard):
        w_copy(5, way, step, chunk, shard, q_x, to_x).wait_recv()

        @pl.when(core == 0)
        def _():
            w_copy(7, way, step, chunk, shard, q_x, to_y).start()

        w_copy(2, way, step, chunk, shard, q_x, to_core).start()
        w_copy(6, way, step, chunk, shard, q_y, to_y).wait_recv()

        @pl.when(core == 1)
        def _():
            w_copy(7, way, step, chunk, shard, q_y, to_x).start()

        w_copy(3, way, step, chunk, shard, q_y, to_core).start()

    def stage_c(way, step, chunk, shard):
        w_copy(7, way, step, chunk, shard, q_d, to_y).wait_recv()
        w_copy(4, way, step, chunk, shard, q_d, to_core).start()

    def multiply(shard, chunk):
        width = cells.shape[3]

        def planes(half, carry):
            parts = []
            for step_y in (-1, 0, 1):
                for step_z in (-1, 0, 1):
                    part = shifted[
                        step_y + 1, shard, pl.ds(half * 2 + 2 - chunk, 2),
                        pl.ds((1 - step_z) * ny, main),
                    ]
                    parts.append(part.reshape(2 * main, width))
            taps = w_all[shard, pl.ds(pl.multiple_of(chunk * chunk_rows, chunk_rows), chunk_rows)]
            product = jnp.dot(
                jnp.concatenate(parts, axis=1), taps, preferred_element_type=jnp.float32
            )
            acc[pl.ds(half * 2, 2)] += product.reshape(2, main, out_ref.shape[2])
            return carry

        lax.fori_loop(0, nx // 2, planes, 0)

    def compute(way, step, chunk, shard):
        @pl.when(chunk == 0)
        def _():
            end_halo(way, step, shard)

        for kind in range(4):
            w_copy(
                1 + kind, way, step, chunk, shard, partner_pieces[kind], to_core
            ).wait_recv()
        multiply(shard, chunk)

    def run(unit, stage):
        step, chunk = 1 + unit // CHUNKS, unit % CHUNKS
        each_arrival(step, lambda way, step, shard: stage(way, step, chunk, shard))

    def g_arrived(way, step, shard):
        g_arrival(way, step).wait_recv()
        start_halo(way, step, shard)

    own_g.wait()
    start_halo(0, 0, z)
    own_w.wait()
    end_halo(0, 0, z)

    def turn(k, carry):
        @pl.when(k < units)
        def _():
            run(k, stage_a)

        @pl.when((k % 2 == 0) & (k // 2 + 1 < n))
        def _():
            step = k // 2 + 1
            for way in (0, 1):
                @pl.when(sends_on(way, step))
                def _():
                    g_copy(way, step).start()

        @pl.when((k >= 1) & (k < units + 1))
        def _():
            run(k - 1, stage_b)

        @pl.when((k >= 2) & (k < units + 2))
        def _():
            run(k - 2, stage_c)

        @pl.when((k < units) & (k % CHUNKS == CHUNKS - 1))
        def _():
            each_arrival(1 + k // CHUNKS, g_arrived)

        @pl.when(k < CHUNKS)
        def _():
            multiply(z, k)

        @pl.when(k >= 3)
        def _():
            run(k - 3, compute)

        return carry

    lax.fori_loop(0, units + 3, turn, 0)
    out_ref[...] = acc[...].astype(out_ref.dtype)

    def end_sends(way, step, chunk, shard):
        w_copy(5, way, step, chunk, shard, q, to_x).wait_send()
        w_copy(6, way, step, chunk, shard, q, to_y).wait_send()
        for kind in range(4):
            w_copy(1 + kind, way, step, chunk, shard, pieces[kind], to_core).wait_send()

        @pl.when(core == 0)
        def _():
            w_copy(7, way, step, chunk, shard, q_x, to_y).wait_send()

        @pl.when(core == 1)
        def _():
            w_copy(7, way, step, chunk, shard, q_y, to_x).wait_send()

        @pl.when((step < n - 1) & sends_on(way, 1))
        def _():
            w_copy(0, way, step + 1, chunk, shard, q, {"chan": z + 1 - 2 * way}).wait_send()

        @pl.when(chunk == 0)
        def _():
            end_halo_sends(way, step, shard)

    def end_halo_sends(way, step, shard):
        h_copy(0, way, step, shard, True).wait_send()

        @pl.when(has_cross)
        def _():
            h_copy(1, way, step, shard, True).wait_send()

    end_halo_sends(0, 0, z)

    def close(unit, carry):
        run(unit, end_sends)
        return carry

    lax.fori_loop(0, units, close, 0)
    for way in (0, 1):
        @pl.when(sends_on(way, 1))
        def _():
            for chunk in range(CHUNKS):
                own_z_copy(way, chunk).wait_send()
        for step in range(1, n):
            @pl.when(sends_on(way, step))
            def _():
                g_copy(way, step).wait_send()


def body_gather(n, ns, grad_out, conv_weight, pre_act, down_weight):
    channels, nx, plane = grad_out.shape
    rows_y = plane // NZ
    ny = rows_y // n
    wide = conv_weight.shape[2]
    main = NZ * ny
    turned = grad_out.reshape(channels, nx, rows_y, NZ).transpose(1, 3, 2, 0)
    edged = jnp.pad(turned, ((0, 0), (0, 0), (1, 1), (0, 0)))
    blocks = turned.reshape(nx, NZ, n, ny, channels).transpose(2, 0, 1, 3, 4)
    blocks = blocks.reshape(n, nx, main, channels)
    low = edged[:, :, 0 : rows_y : ny].transpose(2, 0, 1, 3)
    high = edged[:, :, ny + 1 :: ny].transpose(2, 0, 1, 3)
    send = jnp.concatenate([blocks, low, high], axis=2)
    weights = conv_weight.reshape(-1, wide)
    vmem = pltpu.VMEM
    dma = pltpu.SemaphoreType.DMA
    grad_act = pl.pallas_call(
        functools.partial(conv_kernel, n, ns, nx, ny),
        out_shape=jax.ShapeDtypeStruct((nx, main, wide), jnp.bfloat16),
        in_specs=[pl.BlockSpec(memory_space=pl.ANY)] * 2,
        out_specs=pl.BlockSpec(memory_space=pltpu.VMEM),
        scratch_shapes=[
            vmem((n, weights.shape[0], wide), jnp.bfloat16),
            vmem((n, nx + 2, main + 2 * NZ, channels), jnp.bfloat16),
            vmem((3, n, nx + 2, main + 2 * ny, channels), jnp.bfloat16),
            vmem((nx, main, wide), jnp.float32),
            dma((8, 2, n, CHUNKS)), dma((8, 2, n, CHUNKS)),
            dma((2, n)), dma((2, n)),
            dma((2, 2, n)), dma((2, 2, n)),
            dma((2,)),
        ],
        compiler_params=pltpu.CompilerParams(
            collective_id=0, has_side_effects=True, vmem_limit_bytes=56 * 2**20
        ),
        cost_estimate=pl.CostEstimate(
            flops=2 * 27 * n * channels * nx * main * wide,
            bytes_accessed=8 * 2**20, transcendentals=0,
        ),
    )(send, weights)
    grad_act = grad_act.reshape(nx, NZ, ny, wide).transpose(0, 2, 1, 3).reshape(nx, main, wide)
    return finish_planes(grad_act, pre_act, down_weight)


def solution(mesh):
    in_specs = (
        P("chan", ("groups", "space", "pair"), None),
        P(None, "chan", None),
        P(("groups", "space", "pair"), "chan", None),
        P(),
    )
    out_specs = P(("groups", "space", "pair"), "chan", None, None)
    n, ns = mesh.shape["chan"], mesh.shape["space"]

    def body(grad_out, conv_weight, pre_act, down_weight):
        channels, nx, plane = grad_out.shape
        ny = plane // NZ // n
        fits = channels % 128 == 0 and ny % 16 == 0 and nx % 2 == 0 and ns % 2 == 0
        fits = fits and mesh.shape["groups"] == 2 and mesh.shape["pair"] == 2
        if fits:
            return body_gather(n, ns, grad_out, conv_weight, pre_act, down_weight)
        return body_blocks(grad_out, conv_weight, pre_act, down_weight)

    return jax.shard_map(body, mesh=mesh, in_specs=in_specs, out_specs=out_specs, check_vma=False)
```
